32 devices in a mesh: cfg: 2 (over core), section: 2 (over y), tp: 8 (over z, x).
Axes of the slice: x: 2, y: 2, z: 4, core: 2. Of those that a mesh axis runs over, the one named last changes fastest.
Arguments:
- latent: bfloat16 [512, 6144], replicated, may hold values from -6 to 6
- condition: bfloat16 [2, 6144], P('cfg'), may hold values from -3 to 3
- gain: bfloat16 [2, 6144], P('section'), may hold values from 0.099609375 to 1.8984375
- w_query: bfloat16 [2, 6144, 1024], P('section', None, 'tp'), may hold values from -0.078125 to 0.078125
- w_key: bfloat16 [2, 6144, 1024], P('section', None, 'tp'), may hold values from -0.078125 to 0.078125
- w_value: bfloat16 [2, 6144, 1024], P('section', None, 'tp'), may hold values from -0.078125 to 0.078125
- w_out: bfloat16 [2, 1024, 6144], P('section', 'tp'), may hold values from -0.5 to 0.5
- stale_keys: bfloat16 [2, 2, 512, 1024], P('cfg', 'section', None, 'tp'), may hold values from -150 to 150
- stale_values: bfloat16 [2, 2, 512, 1024], P('cfg', 'section', None, 'tp'), may hold values from -6 to 6
- patch_order: int32 [4], replicated, may hold values from 0 to 3, each once
- stale_mask: int32 [4], replicated, may hold values 0 or 1
Outputs:
- guided: bfloat16 [512, 6144], P(('cfg', 'section'), 'tp')
- new_keys: bfloat16 [2, 2, 512, 1024], P('cfg', 'section', None, 'tp')
- new_values: bfloat16 [2, 2, 512, 1024], P('cfg', 'section', None, 'tp')
The draws below stay inside these ranges and needn't reach their ends.
Inputs may be any that keep to these rules, and one draw needn't show every extreme that they name: `patch_order`: each of the 4 patch numbers exactly once.
All inputs are finite; a program needn't handle non-finite values.
Results may differ from the reference program's by a relative error of at most 0.035.
Values may be sent and summed in bfloat16 or wider, within the bound.
A program may use at most 64 MiB of HBM per device.

```python
import jax
import jax.numpy as jnp
from jax import lax

D = 6144
HEAD_DIM = 128
HEAD_DEV = 1
PATCH_LEN = 128
PATCHES = 4
HEADS = 8
LAYERS = 2
SEQ = 512


def draw_stale_keys(key, part):
    key = jax.random.fold_in(key, 11)
    shape = (2, LAYERS, SEQ, HEADS * HEAD_DIM)
    base = jax.random.normal(key, shape, jnp.float32)
    return jnp.clip(base, -6.0, 6.0).astype(jnp.bfloat16)


def with_ends(result, rng, least, largest):
    extent = result.shape
    place = [jax.random.randint(jax.random.fold_in(rng, axis), (), 0, extent[axis]) for axis in range(len(extent))]
    result = result.at[tuple(place)].set(least)
    longest = extent.index(max(extent))
    place[longest] = (place[longest] + 1) % extent[longest]
    return result.at[tuple(place)].set(largest)


def level_of(key, dims, cuts, smallest, top_value):
    loudness = 1.0
    for dim, blocks in cuts:
        steps = jax.random.uniform(jax.random.fold_in(jax.random.fold_in(key, 6), dim), (blocks,), jnp.float32, smallest / len(cuts), top_value / len(cuts))
        loudness = loudness * jnp.repeat(jnp.exp(steps), dims[dim] // blocks).reshape((-1,) + (1,) * (len(dims) - 1 - dim))
    return loudness


def centred(rng, shape, width, reach, pieces=(), kind=jnp.bfloat16):
    factor_of = level_of(rng, shape, pieces, -0.22, 0.18) if pieces else 1.0
    values = jax.random.normal(rng, shape, jnp.float32) * width * factor_of
    return jnp.minimum(jnp.maximum(values, -reach), reach).astype(kind)


def setup_inputs(seed: int = 0) -> dict:
    seeds = jax.random.split(jax.random.key(seed), 12)
    latent = centred(seeds[0], (SEQ, D), 1.0, 6.0)
    condition = centred(seeds[1], (2, D), 0.5, 3.0, ((0, 2),))
    gain = jnp.clip(1.0 + 0.18 * jax.random.normal(seeds[2], (LAYERS, D), jnp.float32), 0.099609375, 1.8984375).astype(jnp.bfloat16)
    w_query = centred(seeds[3], (LAYERS, D, HEADS * HEAD_DIM), D ** -0.5, 0.078125, ((0, 2), (2, 8)))
    w_key = centred(seeds[4], (LAYERS, D, HEADS * HEAD_DIM), D ** -0.5, 0.078125, ((0, 2), (2, 8)))
    w_value = centred(seeds[5], (LAYERS, D, HEADS * HEAD_DIM), D ** -0.5, 0.078125, ((0, 2), (2, 8)))
    w_out = centred(seeds[6], (LAYERS, HEADS * HEAD_DIM, D), HEAD_DIM ** -0.5, 0.5, ((0, 2), (1, 8)))
    stale_keys = draw_stale_keys(jax.random.fold_in(seeds[11], 71), 0)
    stale_values = centred(seeds[8], (2, LAYERS, SEQ, HEADS * HEAD_DIM), 1.0, 6.0, ((0, 2), (1, 2), (3, 8)))
    patch_order = jax.random.permutation(seeds[9], PATCHES).astype(jnp.int32)
    stale_mask = with_ends((jax.random.randint(seeds[10], (PATCHES,), 0, 4) < 3).astype(jnp.int32), jax.random.fold_in(seeds[10], 1), 0, 1)
    return dict(latent=latent, condition=condition, gain=gain, w_query=w_query, w_key=w_key, w_value=w_value, w_out=w_out, stale_keys=stale_keys, stale_values=stale_values, patch_order=patch_order, stale_mask=stale_mask)


GUIDE_SCALE = 3.0
NORM_EPS = 1e-06

def token_positions(patch_order, stale_mask):
    numbers = jnp.arange(PATCHES, dtype=jnp.int32)
    placed = lax.optimization_barrier(jnp.sum(numbers[:, None] * (patch_order[:, None] == numbers[None, :]).astype(jnp.int32), axis=0))
    return (jnp.repeat(placed, PATCH_LEN), jnp.repeat(stale_mask, PATCH_LEN) == 1)

def attend_head(query, fresh_keys, fresh_values, old_keys, old_values, fresh_open, stale_open):
    factor = HEAD_DIM ** (-0.5)
    fresh_scores = jnp.where(fresh_open, jnp.dot(query, fresh_keys.T, preferred_element_type=jnp.float32) * factor, -jnp.inf)
    old_scores = jnp.where(stale_open, jnp.dot(query, old_keys.T, preferred_element_type=jnp.float32) * factor, -jnp.inf)
    top = jnp.maximum(lax.optimization_barrier(jnp.max(fresh_scores, axis=1, keepdims=True)), lax.optimization_barrier(jnp.max(old_scores, axis=1, keepdims=True)))
    fresh_exp = jnp.exp(fresh_scores - top)
    old_exp = jnp.exp(old_scores - top)
    total = lax.optimization_barrier(jnp.sum(fresh_exp, axis=1, keepdims=True)) + lax.optimization_barrier(jnp.sum(old_exp, axis=1, keepdims=True))
    fresh_weight = (fresh_exp / total).astype(jnp.bfloat16)
    old_weight = (old_exp / total).astype(jnp.bfloat16)
    mixed = jnp.dot(fresh_weight, fresh_values, preferred_element_type=jnp.float32) + jnp.dot(old_weight, old_values, preferred_element_type=jnp.float32)
    return mixed.astype(jnp.bfloat16)

def layer(current, gain_row, query_w, key_w, value_w, out_w, old_keys, old_values, key_pos, key_open):
    row_float = current.astype(jnp.float32)
    scaled = row_float * lax.rsqrt(lax.optimization_barrier(jnp.mean(row_float * row_float, axis=1, keepdims=True)) + NORM_EPS)
    normed = (scaled * gain_row.astype(jnp.float32)[None, :]).astype(jnp.bfloat16)
    query = jnp.dot(normed, query_w, preferred_element_type=jnp.float32).astype(jnp.bfloat16)
    keys = jnp.dot(normed, key_w, preferred_element_type=jnp.float32).astype(jnp.bfloat16)
    values = jnp.dot(normed, value_w, preferred_element_type=jnp.float32).astype(jnp.bfloat16)
    fresh_open = key_pos[None, :] <= key_pos[:, None]
    stale_open = (key_pos[None, :] > key_pos[:, None]) & key_open[None, :]

    def split(array):
        return array.reshape(SEQ, HEADS, HEAD_DIM).transpose(1, 0, 2)

    def one_head(item):
        head_query, head_keys, head_values, head_old_keys, head_old_values = item
        return attend_head(head_query, head_keys, head_values, head_old_keys, head_old_values, fresh_open, stale_open)
    mixed = lax.map(one_head, (split(query), split(keys), split(values), split(old_keys), split(old_values)))
    attention = mixed.transpose(1, 0, 2).reshape(SEQ, HEADS * HEAD_DIM)
    group_width = HEAD_DEV * HEAD_DIM
    group_count = HEADS // HEAD_DEV
    parts = attention.reshape(SEQ, group_count, group_width).transpose(1, 0, 2)
    out_rows = out_w.reshape(group_count, group_width, D)

    def accumulate(total, item):
        part, weight = item
        term = jnp.dot(part, weight, preferred_element_type=jnp.float32).astype(jnp.bfloat16)
        return (total + lax.optimization_barrier(term).astype(jnp.float32), None)
    summed, _ = lax.scan(accumulate, jnp.zeros((SEQ, D), jnp.float32), (parts, out_rows))
    return ((row_float + summed).astype(jnp.bfloat16), keys, values)

def reference(latent, condition, gain, w_query, w_key, w_value, w_out, stale_keys, stale_values, patch_order, stale_mask):
    key_pos, key_open = token_positions(patch_order, stale_mask)
    finals = []
    keys_all = []
    values_all = []
    for branch in range(2):
        current = (latent.astype(jnp.float32) + condition[branch].astype(jnp.float32)[None, :]).astype(jnp.bfloat16)
        branch_keys = []
        branch_values = []
        for level in range(LAYERS):
            current, keys, values = layer(current, gain[level], w_query[level], w_key[level], w_value[level], w_out[level], stale_keys[branch, level], stale_values[branch, level], key_pos, key_open)
            branch_keys.append(keys)
            branch_values.append(values)
        finals.append(current)
        keys_all.append(jnp.stack(branch_keys))
        values_all.append(jnp.stack(branch_values))
    conditioned = finals[0].astype(jnp.float32)
    unconditioned = finals[1].astype(jnp.float32)
    guided = (unconditioned + GUIDE_SCALE * (conditioned - unconditioned)).astype(jnp.bfloat16)
    return (guided, jnp.stack(keys_all), jnp.stack(values_all))
```

```python
import jax
import jax.numpy as jnp
from jax import lax
from jax.sharding import PartitionSpec as P

HEAD_DIM = 128
PATCH_LEN = 128
PATCHES = 4


GUIDE_SCALE = 3.0
NORM_EPS = 1e-06


def passed_along(block, axis, distance):
    devices = range(lax.axis_size(axis))
    route = [((i - distance) % len(devices), i) for i in devices]
    return lax.ppermute(block, axis, route)


def partner_2(x, axis, stride):
    return lax.ppermute(x, axis, [(i, i ^ 1 << stride) for i in range(lax.axis_size(axis))])


def attend_rows(query, fresh_keys, fresh_values, old_keys, old_values, fresh_open, stale_open):
    row_count = query.shape[0]
    head_count = query.shape[1] // HEAD_DIM
    key_count = fresh_keys.shape[0]
    factor = HEAD_DIM ** (-0.5)
    query_heads = query.reshape(row_count, head_count, HEAD_DIM)

    def split(array):
        return array.reshape(key_count, head_count, HEAD_DIM)

    fresh_scores = (
        jnp.einsum(
            "rhe,she->hrs", query_heads, split(fresh_keys), preferred_element_type=jnp.float32
        )
        * factor
    )
    old_scores = (
        jnp.einsum("rhe,she->hrs", query_heads, split(old_keys), preferred_element_type=jnp.float32)
        * factor
    )
    fresh_scores = jnp.where(fresh_open[None], fresh_scores, -jnp.inf)
    old_scores = jnp.where(stale_open[None], old_scores, -jnp.inf)
    top = jnp.maximum(
        jnp.max(fresh_scores, axis=2, keepdims=True), jnp.max(old_scores, axis=2, keepdims=True)
    )
    fresh_exp = jnp.exp(fresh_scores - top)
    old_exp = jnp.exp(old_scores - top)
    total = jnp.sum(fresh_exp, axis=2, keepdims=True) + jnp.sum(old_exp, axis=2, keepdims=True)
    fresh_weight = (fresh_exp / total).astype(jnp.bfloat16)
    old_weight = (old_exp / total).astype(jnp.bfloat16)
    mixed = jnp.einsum(
        "hrs,she->rhe", fresh_weight, split(fresh_values), preferred_element_type=jnp.float32
    )
    mixed = mixed + jnp.einsum(
        "hrs,she->rhe", old_weight, split(old_values), preferred_element_type=jnp.float32
    )
    return mixed.reshape(row_count, head_count * HEAD_DIM).astype(jnp.bfloat16)


def body(
    latent,
    condition,
    gain,
    w_query,
    w_key,
    w_value,
    w_out,
    stale_keys,
    stale_values,
    patch_order,
    stale_mask,
):
    tp_count = lax.axis_size("tp")
    section_count = lax.axis_size("section")
    section = lax.axis_index("section")
    tp_index = lax.axis_index("tp")
    branch = lax.axis_index("cfg")
    width = latent.shape[1]
    local_width = width // tp_count
    seq_len = latent.shape[0]
    query_w = w_query[0]
    key_w = w_key[0]
    value_w = w_value[0]
    out_w = w_out[0]
    gain_row = gain[0].astype(jnp.float32)
    old_keys = stale_keys[0, 0]
    old_values = stale_values[0, 0]
    numbers = jnp.arange(PATCHES, dtype=jnp.int32)
    placed = jnp.sum(
        numbers[:, None] * (patch_order[:, None] == numbers[None, :]).astype(jnp.int32), axis=0
    )
    pos = jnp.repeat(placed, PATCH_LEN)
    key_open = jnp.repeat(stale_mask, PATCH_LEN) == 1
    fresh_open = pos[None, :] <= pos[:, None]
    stale_open = (pos[None, :] > pos[:, None]) & key_open[None, :]
    entry = (latent.astype(jnp.float32) + condition[0].astype(jnp.float32)[None, :]).astype(
        jnp.bfloat16
    )
    gather_weights = 2 * tp_count * out_w.shape[0] <= seq_len * 4
    if gather_weights:
        first_out = lax.all_gather(passed_along(out_w, "section", 1), "tp", axis=0, tiled=True)

    def project(rows):
        row_float = rows.astype(jnp.float32)
        scaled = row_float * lax.rsqrt(
            jnp.mean(row_float * row_float, axis=1, keepdims=True) + NORM_EPS
        )
        normed = (scaled * gain_row[None, :]).astype(jnp.bfloat16)
        return [
            jnp.dot(normed, w, preferred_element_type=jnp.float32).astype(jnp.bfloat16)
            for w in (query_w, key_w, value_w)
        ]

    query0, keys0, values0 = project(entry)
    mixed0 = attend_rows(query0, keys0, values0, old_keys, old_values, fresh_open, stale_open)
    if gather_weights:
        mixed0 = lax.all_gather(passed_along(mixed0, "section", 1), "tp", axis=1, tiled=True)
        summed = jnp.dot(mixed0, first_out, preferred_element_type=jnp.float32)
        second = (entry.astype(jnp.float32) + summed).astype(jnp.bfloat16)
    else:
        term = jnp.dot(mixed0, out_w, preferred_element_type=jnp.float32)
        summed = lax.psum_scatter(
            term.astype(jnp.bfloat16), "tp", scatter_dimension=1, tiled=True
        ).astype(jnp.float32)
        current = lax.dynamic_slice_in_dim(entry, tp_index * local_width, local_width, 1)
        second = (current.astype(jnp.float32) + summed).astype(jnp.bfloat16)
        second = lax.all_gather(passed_along(second, "section", 1), "tp", axis=1, tiled=True)
    query1, keys1, values1 = project(second)
    mixed1 = attend_rows(query1, keys1, values1, old_keys, old_values, fresh_open, stale_open)
    term = jnp.dot(mixed1, out_w, preferred_element_type=jnp.float32)
    summed = lax.psum_scatter(
        term.astype(jnp.bfloat16), "tp", scatter_dimension=1, tiled=True
    ).astype(jnp.float32)
    current = lax.dynamic_slice_in_dim(second, tp_index * local_width, local_width, 1)
    result = (current.astype(jnp.float32) + summed).astype(jnp.bfloat16)
    quarter = seq_len // 4

    def rows_of(block):
        return lax.dynamic_slice_in_dim(result, block * quarter, quarter, 0)

    pair = jnp.concatenate([rows_of(0), rows_of(2)], axis=0)
    pair = jnp.where(section == 1, jnp.concatenate([rows_of(1), rows_of(3)]), passed_along(pair, "section", 1))
    own_rows = lax.dynamic_slice_in_dim(pair, branch * quarter, quarter, 0)
    outbound = lax.dynamic_slice_in_dim(pair, (1 - branch) * quarter, quarter, 0)
    partner = partner_2(outbound, "cfg", 0)
    conditioned = jnp.where(branch == 0, own_rows, partner).astype(jnp.float32)
    unconditioned = jnp.where(branch == 0, partner, own_rows).astype(jnp.float32)
    guided = (unconditioned + GUIDE_SCALE * (conditioned - unconditioned)).astype(jnp.bfloat16)
    keys = jnp.where(section == 0, keys0, keys1)
    values = jnp.where(section == 0, values0, values1)
    return (guided, keys[None, None], values[None, None])


def solution(mesh):
    placed = (
        P(),
        P("cfg", None),
        P("section", None),
        P("section", None, "tp"),
        P("section", None, "tp"),
        P("section", None, "tp"),
        P("section", "tp", None),
        P("cfg", "section", None, "tp"),
        P("cfg", "section", None, "tp"),
        P(),
        P(),
    )
    return jax.shard_map(
        body,
        mesh=mesh,
        in_specs=placed,
        out_specs=(
            P(("cfg", "section"), "tp"),
            P("cfg", "section", None, "tp"),
            P("cfg", "section", None, "tp"),
        ),
        check_vma=False,
    )
```

```python
import jax
import jax.numpy as jnp
from jax import lax
from jax.experimental import pallas as pl
from jax.experimental.pallas import tpu as pltpu
from jax.sharding import PartitionSpec as P

HEAD_DIM = 128
PATCH_LEN = 128
PATCHES = 4


GUIDE_SCALE = 3.0
NORM_EPS = 1e-06


def passed_along(block, axis, distance):
    devices = range(lax.axis_size(axis))
    route = [((i - distance) % len(devices), i) for i in devices]
    return lax.ppermute(block, axis, route)


def partner_2(x, axis, stride):
    return lax.ppermute(x, axis, [(i, i ^ 1 << stride) for i in range(lax.axis_size(axis))])


def attend_rows(query, fresh_keys, fresh_values, old_keys, old_values, fresh_open, stale_open):
    row_count = query.shape[0]
    head_count = query.shape[1] // HEAD_DIM
    key_count = fresh_keys.shape[0]
    factor = HEAD_DIM ** (-0.5)
    query_heads = query.reshape(row_count, head_count, HEAD_DIM)

    def split(array):
        return array.reshape(key_count, head_count, HEAD_DIM)

    fresh_scores = (
        jnp.einsum(
            "rhe,she->hrs", query_heads, split(fresh_keys), preferred_element_type=jnp.float32
        )
        * factor
    )
    old_scores = (
        jnp.einsum("rhe,she->hrs", query_heads, split(old_keys), preferred_element_type=jnp.float32)
        * factor
    )
    fresh_scores = jnp.where(fresh_open[None], fresh_scores, -jnp.inf)
    old_scores = jnp.where(stale_open[None], old_scores, -jnp.inf)
    top = jnp.maximum(
        jnp.max(fresh_scores, axis=2, keepdims=True), jnp.max(old_scores, axis=2, keepdims=True)
    )
    fresh_exp = jnp.exp(fresh_scores - top)
    old_exp = jnp.exp(old_scores - top)
    total = jnp.sum(fresh_exp, axis=2, keepdims=True) + jnp.sum(old_exp, axis=2, keepdims=True)
    fresh_weight = (fresh_exp / total).astype(jnp.bfloat16)
    old_weight = (old_exp / total).astype(jnp.bfloat16)
    mixed = jnp.einsum(
        "hrs,she->rhe", fresh_weight, split(fresh_values), preferred_element_type=jnp.float32
    )
    mixed = mixed + jnp.einsum(
        "hrs,she->rhe", old_weight, split(old_values), preferred_element_type=jnp.float32
    )
    return mixed.reshape(row_count, head_count * HEAD_DIM).astype(jnp.bfloat16)


GRID_X = 2
LINE = 4
MESH = pl.DeviceIdType.MESH


def span(index, size):
    return pl.ds(pl.multiple_of(index * size, size), size)


def arrived(ref, sem):
    pltpu.make_async_copy(ref, ref, sem).wait()


def greet(targets):
    barrier = pltpu.get_barrier_semaphore()
    for target in targets:
        pl.semaphore_signal(barrier, inc=1, device_id=target, device_id_type=MESH)
    pl.semaphore_wait(barrier, len(targets))


def send(src, dst, send_sem, recv_sem, target):
    copy = pltpu.make_async_remote_copy(
        src_ref=src,
        dst_ref=dst,
        send_sem=send_sem,
        recv_sem=recv_sem,
        device_id=target,
        device_id_type=MESH,
    )
    copy.start()
    return copy


def share_kernel(
    w_out,
    w_query,
    w_key,
    w_value,
    mixed,
    wo,
    heads,
    proj,
    cols,
    wo_recv,
    wo_send,
    heads_recv,
    heads_send,
    proj_recv,
    proj_send,
    cols_recv,
    cols_send,
    edge_sem,
    local_sem,
):
    c = lax.axis_index("cfg")
    s = lax.axis_index("section")
    t = lax.axis_index("tp")
    tp = GRID_X * LINE
    half = wo.shape[1]
    part = half // 2
    head = mixed.shape[1]
    slim = cols.shape[1] // 2
    across = t + 1 - 2 * lax.rem(t, 2)
    peers = [lax.rem(t + GRID_X * k, tp) for k in range(1, LINE)]
    sibling = {"cfg": 1 - c}
    other = {"section": 1 - s}
    greet([{"tp": lax.rem(t + k, tp)} for k in range(1, tp)] + [sibling, other])
    weights = (w_query, w_key, w_value)

    def wo_at(core, index):
        return wo.at[span(index, head), span(core, part)]

    def heads_at(index):
        return heads.at[:, span(index, head)]

    def cols_at(core, index):
        return cols.at[span(index, head), span(core, slim)]

    def proj_at(core, j):
        return proj.at[span(core, part), j * head : (j + 1) * head]

    def edge(j):
        return edge_sem.at[j]

    first_head = (mixed, heads_at(t))
    first_wo = (w_out.at[:, span(c, part)], wo_at(c, t))

    @pl.when(s == 0)
    def _():
        send(mixed, heads_at(t), edge(0), heads_recv.at[t], other)
        send(w_out.at[:, span(c + 2, part)], wo_at(c, t), edge(1), wo_recv.at[c, t], other)
        a = pltpu.make_async_copy(*first_head, local_sem.at[0])
        b = pltpu.make_async_copy(*first_wo, local_sem.at[1])
        a.start()
        b.start()
        a.wait()
        b.wait()

    @pl.when(s == 1)
    def _():
        for j, w in enumerate(weights):
            send(w.at[span(c, part), :], proj_at(c, j), edge(j), proj_recv.at[c, j], other)
        local = [
            pltpu.make_async_copy(
                w.at[half : 2 * half, :], proj.at[:, j * head : (j + 1) * head], local_sem.at[j]
            )
            for j, w in enumerate(weights)
        ]
        local += [
            pltpu.make_async_copy(
                w_out.at[:, pl.ds(pl.multiple_of(2 * slim * t + slim * core, slim), slim)],
                cols_at(core, t),
                local_sem.at[3 + core],
            )
            for core in range(2)
        ]
        for copy in local:
            copy.start()
        arrived(heads_at(t), heads_recv.at[t])
        arrived(wo_at(c, t), wo_recv.at[c, t])
        for copy in local:
            copy.wait()

    pending = []

    def pass_heads(index, slot, target):
        pending.append(
            send(heads_at(index), heads_at(index), heads_send.at[slot], heads_recv.at[index], target)
        )

    def pass_wo(index, slot, target):
        pending.append(
            send(wo_at(c, index), wo_at(c, index), wo_send.at[slot], wo_recv.at[c, index], target)
        )

    for k, peer in enumerate(peers):
        pass_heads(t, k, {"tp": peer})
    pass_heads(t, 3, {"tp": across})
    for k, peer in enumerate(peers):
        pass_wo(t, k, {"tp": peer})
    pass_wo(t, 3, {"tp": across})
    pass_wo(t, 7, sibling)

    @pl.when(s == 1)
    def _():
        for k in range(1, tp):
            to = lax.rem(t + k, tp)
            send(
                w_out.at[:, pl.ds(pl.multiple_of(2 * slim * to + slim * c, slim), slim)],
                cols_at(c, t),
                cols_send.at[k],
                cols_recv.at[c, t],
                {"tp": to},
            )

    @pl.when(s == 0)
    def _():
        for j in range(3):
            arrived(proj_at(c, j), proj_recv.at[c, j])
            send(proj_at(c, j), proj_at(c, j), proj_send.at[j], proj_recv.at[c, j], sibling)

    for k in (2, 0, 1):
        peer = peers[k]
        arrived(heads_at(peer), heads_recv.at[peer])
        pass_heads(peer, 4 + k, {"tp": across})
    for k in (2, 0, 1):
        peer = peers[k]
        arrived(wo_at(c, peer), wo_recv.at[c, peer])
        pass_wo(peer, 4 + k, {"tp": across})
        pass_wo(peer, 8 + k, sibling)
    for k in range(LINE):
        index = lax.rem(across + GRID_X * k, tp)
        arrived(heads_at(index), heads_recv.at[index])
        arrived(wo_at(c, index), wo_recv.at[c, index])
        pass_wo(index, 11 + k, sibling)
    for k in range(tp):
        arrived(wo_at(1 - c, k), wo_recv.at[1 - c, k])

    @pl.when(s == 0)
    def _():
        for j in range(3):
            arrived(proj_at(1 - c, j), proj_recv.at[1 - c, j])
            arrived(proj_at(c, j), proj_send.at[j])
        arrived(mixed, edge(0))
        arrived(w_out.at[:, span(c + 2, part)], edge(1))

    @pl.when(s == 1)
    def _():
        for k in range(1, tp):
            index = lax.rem(t + k, tp)
            arrived(cols_at(c, index), cols_recv.at[c, index])
            send(
                cols_at(c, index),
                cols_at(c, index),
                cols_send.at[tp + k],
                cols_recv.at[c, index],
                sibling,
            )
        for k in range(1, tp):
            index = lax.rem(t + k, tp)
            arrived(cols_at(1 - c, index), cols_recv.at[1 - c, index])
            arrived(cols_at(c, index), cols_send.at[k])
            arrived(cols_at(c, index), cols_send.at[tp + k])
        for j, w in enumerate(weights):
            arrived(w.at[span(c, part), :], edge(j))

    for copy in pending:
        copy.wait_send()


def share(w_out, w_query, w_key, w_value, mixed):
    head, width = w_out.shape
    tp = GRID_X * LINE
    kind = w_out.dtype
    DMA = pltpu.SemaphoreType.DMA
    any_spec = pl.BlockSpec(memory_space=pl.ANY)
    return pl.pallas_call(
        share_kernel,
        out_shape=(
            jax.ShapeDtypeStruct((tp * head, width // 2), kind),
            jax.ShapeDtypeStruct((mixed.shape[0], tp * head), kind),
            jax.ShapeDtypeStruct((width // 2, 3 * head), kind),
            jax.ShapeDtypeStruct((tp * head, width // tp), kind),
        ),
        in_specs=[any_spec] * 5,
        out_specs=(any_spec,) * 4,
        scratch_shapes=[
            DMA((2, tp)),
            DMA((16,)),
            DMA((tp,)),
            DMA((8,)),
            DMA((2, 3)),
            DMA((3,)),
            DMA((2, tp)),
            DMA((2 * tp,)),
            DMA((3,)),
            DMA((5,)),
        ],
        compiler_params=pltpu.CompilerParams(collective_id=0, has_side_effects=True),
    )(w_out, w_query, w_key, w_value, mixed)


def gather_kernel(mixed, heads, recv, sent, local_sem):
    t = lax.axis_index("tp")
    tp = GRID_X * LINE
    head = mixed.shape[1]
    across = t + 1 - 2 * lax.rem(t, 2)
    peers = [lax.rem(t + GRID_X * k, tp) for k in range(1, LINE)]
    greet([{"tp": p} for p in peers] + [{"tp": across}])

    def heads_at(index):
        return heads.at[:, span(index, head)]

    local = pltpu.make_async_copy(mixed, heads_at(t), local_sem)
    local.start()
    pending = []
    for k, peer in enumerate(peers):
        pending.append(send(mixed, heads_at(t), sent.at[k], recv.at[t], {"tp": peer}))
    pending.append(send(mixed, heads_at(t), sent.at[3], recv.at[t], {"tp": across}))
    for k in (2, 0, 1):
        peer = peers[k]
        arrived(heads_at(peer), recv.at[peer])
        pending.append(
            send(heads_at(peer), heads_at(peer), sent.at[4 + k], recv.at[peer], {"tp": across})
        )
    for k in range(LINE):
        index = lax.rem(across + GRID_X * k, tp)
        arrived(heads_at(index), recv.at[index])
    local.wait()
    for copy in pending:
        copy.wait_send()


def gather_heads(mixed):
    tp = GRID_X * LINE
    DMA = pltpu.SemaphoreType.DMA
    return pl.pallas_call(
        gather_kernel,
        out_shape=jax.ShapeDtypeStruct((mixed.shape[0], tp * mixed.shape[1]), mixed.dtype),
        in_specs=[pl.BlockSpec(memory_space=pltpu.VMEM)],
        out_specs=pl.BlockSpec(memory_space=pltpu.VMEM),
        scratch_shapes=[DMA((tp,)), DMA((8,)), DMA],
        compiler_params=pltpu.CompilerParams(
            collective_id=1, has_side_effects=True, vmem_limit_bytes=16 * 1024 * 1024
        ),
    )(mixed)


def body(
    latent,
    condition,
    gain,
    w_query,
    w_key,
    w_value,
    w_out,
    stale_keys,
    stale_values,
    patch_order,
    stale_mask,
):
    tp_count = lax.axis_size("tp")
    section_count = lax.axis_size("section")
    section = lax.axis_index("section")
    tp_index = lax.axis_index("tp")
    branch = lax.axis_index("cfg")
    width = latent.shape[1]
    local_width = width // tp_count
    seq_len = latent.shape[0]
    query_w = w_query[0]
    key_w = w_key[0]
    value_w = w_value[0]
    out_w = w_out[0]
    gain_row = gain[0].astype(jnp.float32)
    old_keys = stale_keys[0, 0]
    old_values = stale_values[0, 0]
    numbers = jnp.arange(PATCHES, dtype=jnp.int32)
    placed = jnp.sum(
        numbers[:, None] * (patch_order[:, None] == numbers[None, :]).astype(jnp.int32), axis=0
    )
    pos = jnp.repeat(placed, PATCH_LEN)
    key_open = jnp.repeat(stale_mask, PATCH_LEN) == 1
    fresh_open = pos[None, :] <= pos[:, None]
    stale_open = (pos[None, :] > pos[:, None]) & key_open[None, :]
    entry = (latent.astype(jnp.float32) + condition[0].astype(jnp.float32)[None, :]).astype(
        jnp.bfloat16
    )
    planned = tp_count == GRID_X * LINE

    def project(rows):
        row_float = rows.astype(jnp.float32)
        scaled = row_float * lax.rsqrt(
            jnp.mean(row_float * row_float, axis=1, keepdims=True) + NORM_EPS
        )
        normed = (scaled * gain_row[None, :]).astype(jnp.bfloat16)
        return [
            jnp.dot(normed, w, preferred_element_type=jnp.float32).astype(jnp.bfloat16)
            for w in (query_w, key_w, value_w)
        ]

    query0, keys0, values0 = project(entry)
    mixed0 = attend_rows(query0, keys0, values0, old_keys, old_values, fresh_open, stale_open)
    if planned:
        half = width // 2
        later_gain = jnp.where(section == 0, passed_along(gain[0], "section", 1), gain[0])
        half_gain = lax.dynamic_slice_in_dim(later_gain, section * half, half, 0)
        out_half, heads0, weights_half, out_cols = share(out_w, query_w, key_w, value_w, mixed0)
        entry_half = lax.dynamic_slice_in_dim(entry, section * half, half, 1)
        second = (
            entry_half.astype(jnp.float32)
            + jnp.dot(heads0, out_half, preferred_element_type=jnp.float32)
        ).astype(jnp.bfloat16)
        second_float = second.astype(jnp.float32)
        squares = jnp.sum(second_float * second_float, axis=1)
        geared = (second_float * half_gain.astype(jnp.float32)[None, :]).astype(jnp.bfloat16)
        partial = jnp.dot(geared, weights_half, preferred_element_type=jnp.float32)
        far_partial = passed_along(partial.astype(jnp.bfloat16), "section", 1)
        far_squares = passed_along(squares, "section", 1)
        scale = lax.rsqrt((squares + far_squares) / width + NORM_EPS)
        projected = ((partial + far_partial.astype(jnp.float32)) * scale[:, None]).astype(
            jnp.bfloat16
        )
        query1, keys1, values1 = jnp.split(projected, 3, axis=1)
        place = lax.rem(tp_index, tp_count // 2)
        current = lax.dynamic_slice_in_dim(second, place * local_width, local_width, 1)
        current = jnp.where(
            tp_index < tp_count // 2, passed_along(current, "section", 1), current
        )
        mixed1 = attend_rows(query1, keys1, values1, old_keys, old_values, fresh_open, stale_open)
        summed = jnp.dot(gather_heads(mixed1), out_cols, preferred_element_type=jnp.float32)
    else:
        term = jnp.dot(mixed0, out_w, preferred_element_type=jnp.float32)
        summed = lax.psum_scatter(
            term.astype(jnp.bfloat16), "tp", scatter_dimension=1, tiled=True
        ).astype(jnp.float32)
        current = lax.dynamic_slice_in_dim(entry, tp_index * local_width, local_width, 1)
        second = (current.astype(jnp.float32) + summed).astype(jnp.bfloat16)
        current = passed_along(second, "section", 1)
        second = lax.all_gather(current, "tp", axis=1, tiled=True)
        query1, keys1, values1 = project(second)
        mixed1 = attend_rows(query1, keys1, values1, old_keys, old_values, fresh_open, stale_open)
        term = jnp.dot(mixed1, out_w, preferred_element_type=jnp.float32)
        summed = lax.psum_scatter(
            term.astype(jnp.bfloat16), "tp", scatter_dimension=1, tiled=True
        ).astype(jnp.float32)
    result = (current.astype(jnp.float32) + summed).astype(jnp.bfloat16)
    quarter = seq_len // 4

    def rows_of(block):
        return lax.dynamic_slice_in_dim(result, block * quarter, quarter, 0)

    pair = jnp.concatenate([rows_of(0), rows_of(2)], axis=0)
    pair = jnp.where(section == 1, jnp.concatenate([rows_of(1), rows_of(3)]), passed_along(pair, "section", 1))
    own_rows = lax.dynamic_slice_in_dim(pair, branch * quarter, quarter, 0)
    outbound = lax.dynamic_slice_in_dim(pair, (1 - branch) * quarter, quarter, 0)
    partner = partner_2(outbound, "cfg", 0)
    conditioned = jnp.where(branch == 0, own_rows, partner).astype(jnp.float32)
    unconditioned = jnp.where(branch == 0, partner, own_rows).astype(jnp.float32)
    guided = (unconditioned + GUIDE_SCALE * (conditioned - unconditioned)).astype(jnp.bfloat16)
    keys = jnp.where(section == 0, keys0, keys1)
    values = jnp.where(section == 0, values0, values1)
    return (guided, keys[None, None], values[None, None])


def solution(mesh):
    placed = (
        P(),
        P("cfg", None),
        P("section", None),
        P("section", None, "tp"),
        P("section", None, "tp"),
        P("section", None, "tp"),
        P("section", "tp", None),
        P("cfg", "section", None, "tp"),
        P("cfg", "section", None, "tp"),
        P(),
        P(),
    )
    return jax.shard_map(
        body,
        mesh=mesh,
        in_specs=placed,
        out_specs=(
            P(("cfg", "section"), "tp"),
            P("cfg", "section", None, "tp"),
            P("cfg", "section", None, "tp"),
        ),
        check_vma=False,
    )
```

```python
import jax
import jax.numpy as jnp
from jax import lax
from jax.experimental import pallas as pl
from jax.experimental.pallas import tpu as pltpu
from jax.sharding import PartitionSpec as P

HEAD_DIM = 128
PATCH_LEN = 128
PATCHES = 4


GUIDE_SCALE = 3.0
NORM_EPS = 1e-06


def passed_along(block, axis, distance):
    devices = range(lax.axis_size(axis))
    route = [((i - distance) % len(devices), i) for i in devices]
    return lax.ppermute(block, axis, route)


def partner_2(x, axis, stride):
    return lax.ppermute(x, axis, [(i, i ^ 1 << stride) for i in range(lax.axis_size(axis))])


def attend_rows(query, fresh_keys, fresh_values, old_keys, old_values, fresh_open, stale_open):
    row_count = query.shape[0]
    head_count = query.shape[1] // HEAD_DIM
    key_count = fresh_keys.shape[0]
    factor = HEAD_DIM ** (-0.5)
    query_heads = query.reshape(row_count, head_count, HEAD_DIM)

    def split(array):
        return array.reshape(key_count, head_count, HEAD_DIM)

    fresh_scores = (
        jnp.einsum(
            "rhe,she->hrs", query_heads, split(fresh_keys), preferred_element_type=jnp.float32
        )
        * factor
    )
    old_scores = (
        jnp.einsum("rhe,she->hrs", query_heads, split(old_keys), preferred_element_type=jnp.float32)
        * factor
    )
    fresh_scores = jnp.where(fresh_open[None], fresh_scores, -jnp.inf)
    old_scores = jnp.where(stale_open[None], old_scores, -jnp.inf)
    top = jnp.maximum(
        jnp.max(fresh_scores, axis=2, keepdims=True), jnp.max(old_scores, axis=2, keepdims=True)
    )
    fresh_exp = jnp.exp(fresh_scores - top)
    old_exp = jnp.exp(old_scores - top)
    total = jnp.sum(fresh_exp, axis=2, keepdims=True) + jnp.sum(old_exp, axis=2, keepdims=True)
    fresh_weight = (fresh_exp / total).astype(jnp.bfloat16)
    old_weight = (old_exp / total).astype(jnp.bfloat16)
    mixed = jnp.einsum(
        "hrs,she->rhe", fresh_weight, split(fresh_values), preferred_element_type=jnp.float32
    )
    mixed = mixed + jnp.einsum(
        "hrs,she->rhe", old_weight, split(old_values), preferred_element_type=jnp.float32
    )
    return mixed.reshape(row_count, head_count * HEAD_DIM).astype(jnp.bfloat16)


GRID_X = 2
LINE = 4
MESH = pl.DeviceIdType.MESH


def span(index, size):
    return pl.ds(pl.multiple_of(index * size, size), size)


def arrived(ref, sem):
    pltpu.make_async_copy(ref, ref, sem).wait()


def greet(targets):
    barrier = pltpu.get_barrier_semaphore()
    for target in targets:
        pl.semaphore_signal(barrier, inc=1, device_id=target, device_id_type=MESH)
    pl.semaphore_wait(barrier, len(targets))


def send(src, dst, send_sem, recv_sem, target):
    copy = pltpu.make_async_remote_copy(
        src_ref=src,
        dst_ref=dst,
        send_sem=send_sem,
        recv_sem=recv_sem,
        device_id=target,
        device_id_type=MESH,
    )
    copy.start()
    return copy


def share_kernel(
    w_out,
    w_query,
    w_key,
    w_value,
    mixed,
    wo,
    heads,
    proj,
    cols,
    wo_recv,
    wo_send,
    heads_recv,
    heads_send,
    proj_recv,
    proj_send,
    cols_recv,
    cols_send,
    edge_sem,
    local_sem,
):
    c = lax.axis_index("cfg")
    s = lax.axis_index("section")
    t = lax.axis_index("tp")
    tp = GRID_X * LINE
    half = wo.shape[1]
    part = half // 2
    head = mixed.shape[1]
    slim = cols.shape[2]
    across = t + 1 - 2 * lax.rem(t, 2)
    peers = [lax.rem(t + GRID_X * k, tp) for k in range(1, LINE)]
    sibling = {"cfg": 1 - c}
    other = {"section": 1 - s}
    greet([{"tp": lax.rem(t + k, tp)} for k in range(1, tp)] + [sibling, other])
    weights = (w_query, w_key, w_value)

    def wo_at(core, index):
        return wo.at[span(index, head), span(core, part)]

    def heads_at(index):
        return heads.at[index]

    def cols_at(core, index):
        return cols.at[core, span(index, head), :]

    def proj_at(core, j):
        return proj.at[j, span(core, part), :]

    def edge(j):
        return edge_sem.at[j]

    first_head = (mixed, heads_at(t))
    first_wo = (w_out.at[:, span(c, part)], wo_at(c, t))

    @pl.when(s == 0)
    def _():
        send(mixed, heads_at(t), edge(0), heads_recv.at[t], other)
        send(w_out.at[:, span(c + 2, part)], wo_at(c, t), edge(1), wo_recv.at[c, t], other)
        a = pltpu.make_async_copy(*first_head, local_sem.at[0])
        b = pltpu.make_async_copy(*first_wo, local_sem.at[1])
        a.start()
        b.start()
        a.wait()
        b.wait()

    def own_copies():
        copies = [
            pltpu.make_async_copy(
                w.at[half : 2 * half, :], proj.at[j], local_sem.at[j]
            )
            for j, w in enumerate(weights)
        ]
        copies += [
            pltpu.make_async_copy(
                w_out.at[:, pl.ds(pl.multiple_of(2 * slim * t + slim * core, slim), slim)],
                cols_at(core, t),
                local_sem.at[3 + core],
            )
            for core in range(2)
        ]
        return copies

    @pl.when(s == 1)
    def _():
        for j, w in enumerate(weights):
            send(w.at[span(c, part), :], proj_at(c, j), edge(j), proj_recv.at[c, j], other)
        for k in range(1, tp):
            to = lax.rem(t + k, tp)
            send(
                w_out.at[:, pl.ds(pl.multiple_of(2 * slim * to + slim * c, slim), slim)],
                cols_at(c, t),
                cols_send.at[k],
                cols_recv.at[c, t],
                {"tp": to},
            )
        for copy in own_copies():
            copy.start()
        arrived(heads_at(t), heads_recv.at[t])
        arrived(wo_at(c, t), wo_recv.at[c, t])

    pending = []

    def pass_heads(index, slot, target):
        pending.append(
            send(heads_at(index), heads_at(index), heads_send.at[slot], heads_recv.at[index], target)
        )

    def pass_wo(index, slot, target):
        pending.append(
            send(wo_at(c, index), wo_at(c, index), wo_send.at[slot], wo_recv.at[c, index], target)
        )

    for k, peer in enumerate(peers):
        pass_heads(t, k, {"tp": peer})
    pass_heads(t, 3, {"tp": across})
    for k, peer in enumerate(peers):
        pass_wo(t, k, {"tp": peer})
    pass_wo(t, 3, {"tp": across})
    pass_wo(t, 7, sibling)

    for k in (2, 0, 1):
        peer = peers[k]
        arrived(heads_at(peer), heads_recv.at[peer])
        pass_heads(peer, 4 + k, {"tp": across})
    for k in (2, 0, 1):
        peer = peers[k]
        arrived(wo_at(c, peer), wo_recv.at[c, peer])
        pass_wo(peer, 4 + k, {"tp": across})
        pass_wo(peer, 8 + k, sibling)
    for k in range(LINE):
        index = lax.rem(across + GRID_X * k, tp)
        arrived(heads_at(index), heads_recv.at[index])
        arrived(wo_at(c, index), wo_recv.at[c, index])
        pass_wo(index, 11 + k, sibling)

    @pl.when(s == 0)
    def _():
        for j in range(3):
            arrived(proj_at(c, j), proj_recv.at[c, j])
            send(proj_at(c, j), proj_at(c, j), proj_send.at[j], proj_recv.at[c, j], sibling)
        for j in range(3):
            arrived(proj_at(1 - c, j), proj_recv.at[1 - c, j])
            arrived(proj_at(c, j), proj_send.at[j])
        arrived(mixed, edge(0))
        arrived(w_out.at[:, span(c + 2, part)], edge(1))

    @pl.when(s == 1)
    def _():
        for k in range(1, tp):
            index = lax.rem(t + k, tp)
            arrived(cols_at(c, index), cols_recv.at[c, index])
            send(
                cols_at(c, index),
                cols_at(c, index),
                cols_send.at[tp + k],
                cols_recv.at[c, index],
                sibling,
            )
        for k in range(1, tp):
            index = lax.rem(t + k, tp)
            arrived(cols_at(1 - c, index), cols_recv.at[1 - c, index])
            arrived(cols_at(c, index), cols_send.at[k])
            arrived(cols_at(c, index), cols_send.at[tp + k])
        for j, w in enumerate(weights):
            arrived(w.at[span(c, part), :], edge(j))
        for copy in own_copies():
            copy.wait()

    for k in range(tp):
        arrived(wo_at(1 - c, k), wo_recv.at[1 - c, k])
    for copy in pending:
        copy.wait_send()


def share(w_out, w_query, w_key, w_value, mixed):
    head, width = w_out.shape
    tp = GRID_X * LINE
    kind = w_out.dtype
    DMA = pltpu.SemaphoreType.DMA
    any_spec = pl.BlockSpec(memory_space=pl.ANY)
    return pl.pallas_call(
        share_kernel,
        out_shape=(
            jax.ShapeDtypeStruct((tp * head, width // 2), kind),
            jax.ShapeDtypeStruct((tp,) + mixed.shape, kind),
            jax.ShapeDtypeStruct((3, width // 2, head), kind),
            jax.ShapeDtypeStruct((2, tp * head, width // tp // 2), kind),
        ),
        in_specs=[any_spec] * 5,
        out_specs=(any_spec,) * 4,
        scratch_shapes=[
            DMA((2, tp)),
            DMA((16,)),
            DMA((tp,)),
            DMA((8,)),
            DMA((2, 3)),
            DMA((3,)),
            DMA((2, tp)),
            DMA((2 * tp,)),
            DMA((3,)),
            DMA((5,)),
        ],
        compiler_params=pltpu.CompilerParams(collective_id=0, has_side_effects=True),
    )(w_out, w_query, w_key, w_value, mixed)


def gather_kernel(mixed, heads, recv, sent, local_sem):
    t = lax.axis_index("tp")
    tp = GRID_X * LINE
    head = mixed.shape[1]
    across = t + 1 - 2 * lax.rem(t, 2)
    peers = [lax.rem(t + GRID_X * k, tp) for k in range(1, LINE)]
    greet([{"tp": p} for p in peers] + [{"tp": across}])

    def heads_at(index):
        return heads.at[:, span(index, head)]

    local = pltpu.make_async_copy(mixed, heads_at(t), local_sem)
    local.start()
    pending = []
    for k, peer in enumerate(peers):
        pending.append(send(mixed, heads_at(t), sent.at[k], recv.at[t], {"tp": peer}))
    pending.append(send(mixed, heads_at(t), sent.at[3], recv.at[t], {"tp": across}))
    for k in (2, 0, 1):
        peer = peers[k]
        arrived(heads_at(peer), recv.at[peer])
        pending.append(
            send(heads_at(peer), heads_at(peer), sent.at[4 + k], recv.at[peer], {"tp": across})
        )
    for k in range(LINE):
        index = lax.rem(across + GRID_X * k, tp)
        arrived(heads_at(index), recv.at[index])
    local.wait()
    for copy in pending:
        copy.wait_send()


def gather_heads(mixed):
    tp = GRID_X * LINE
    DMA = pltpu.SemaphoreType.DMA
    return pl.pallas_call(
        gather_kernel,
        out_shape=jax.ShapeDtypeStruct((mixed.shape[0], tp * mixed.shape[1]), mixed.dtype),
        in_specs=[pl.BlockSpec(memory_space=pltpu.VMEM)],
        out_specs=pl.BlockSpec(memory_space=pltpu.VMEM),
        scratch_shapes=[DMA((tp,)), DMA((8,)), DMA],
        compiler_params=pltpu.CompilerParams(
            collective_id=1, has_side_effects=True, vmem_limit_bytes=16 * 1024 * 1024
        ),
    )(mixed)


def body(
    latent,
    condition,
    gain,
    w_query,
    w_key,
    w_value,
    w_out,
    stale_keys,
    stale_values,
    patch_order,
    stale_mask,
):
    tp_count = lax.axis_size("tp")
    section_count = lax.axis_size("section")
    section = lax.axis_index("section")
    tp_index = lax.axis_index("tp")
    branch = lax.axis_index("cfg")
    width = latent.shape[1]
    local_width = width // tp_count
    seq_len = latent.shape[0]
    query_w = w_query[0]
    key_w = w_key[0]
    value_w = w_value[0]
    out_w = w_out[0]
    gain_row = gain[0].astype(jnp.float32)
    old_keys = stale_keys[0, 0]
    old_values = stale_values[0, 0]
    numbers = jnp.arange(PATCHES, dtype=jnp.int32)
    placed = jnp.sum(
        numbers[:, None] * (patch_order[:, None] == numbers[None, :]).astype(jnp.int32), axis=0
    )
    pos = jnp.repeat(placed, PATCH_LEN)
    key_open = jnp.repeat(stale_mask, PATCH_LEN) == 1
    fresh_open = pos[None, :] <= pos[:, None]
    stale_open = (pos[None, :] > pos[:, None]) & key_open[None, :]
    entry = (latent.astype(jnp.float32) + condition[0].astype(jnp.float32)[None, :]).astype(
        jnp.bfloat16
    )
    planned = tp_count == GRID_X * LINE

    def project(rows):
        row_float = rows.astype(jnp.float32)
        scaled = row_float * lax.rsqrt(
            jnp.mean(row_float * row_float, axis=1, keepdims=True) + NORM_EPS
        )
        normed = (scaled * gain_row[None, :]).astype(jnp.bfloat16)
        return [
            jnp.dot(normed, w, preferred_element_type=jnp.float32).astype(jnp.bfloat16)
            for w in (query_w, key_w, value_w)
        ]

    query0, keys0, values0 = project(entry)
    mixed0 = attend_rows(query0, keys0, values0, old_keys, old_values, fresh_open, stale_open)
    if planned:
        half = width // 2
        later_gain = jnp.where(section == 0, passed_along(gain[0], "section", 1), gain[0])
        half_gain = lax.dynamic_slice_in_dim(later_gain, section * half, half, 0)
        out_half, heads0, weights_half, out_cols = share(out_w, query_w, key_w, value_w, mixed0)
        entry_half = lax.dynamic_slice_in_dim(entry, section * half, half, 1)
        second = (
            entry_half.astype(jnp.float32)
            + jnp.dot(
                heads0.transpose(1, 0, 2).reshape(seq_len, tp_count * HEAD_DIM),
                out_half,
                preferred_element_type=jnp.float32,
            )
        ).astype(jnp.bfloat16)
        second_float = second.astype(jnp.float32)
        squares = jnp.sum(second_float * second_float, axis=1)
        geared = (second_float * half_gain.astype(jnp.float32)[None, :]).astype(jnp.bfloat16)
        partial = jnp.concatenate(
            [jnp.dot(geared, weights_half[j], preferred_element_type=jnp.float32) for j in range(3)],
            axis=1,
        )
        far_partial = passed_along(partial.astype(jnp.bfloat16), "section", 1)
        far_squares = passed_along(squares, "section", 1)
        scale = lax.rsqrt((squares + far_squares) / width + NORM_EPS)
        projected = ((partial + far_partial.astype(jnp.float32)) * scale[:, None]).astype(
            jnp.bfloat16
        )
        query1, keys1, values1 = jnp.split(projected, 3, axis=1)
        place = lax.rem(tp_index, tp_count // 2)
        current = lax.dynamic_slice_in_dim(second, place * local_width, local_width, 1)
        current = jnp.where(
            tp_index < tp_count // 2, passed_along(current, "section", 1), current
        )
        mixed1 = attend_rows(query1, keys1, values1, old_keys, old_values, fresh_open, stale_open)
        rows = seq_len // 2

        def both(array):
            mine = lax.dynamic_slice_in_dim(array, branch * rows, rows, 0)
            away = lax.dynamic_slice_in_dim(array, (1 - branch) * rows, rows, 0)
            away = partner_2(away, "cfg", 0).astype(jnp.float32)
            mine = mine.astype(jnp.float32)
            cond = jnp.where(branch == 0, mine, away)
            uncond = jnp.where(branch == 0, away, mine)
            return uncond + GUIDE_SCALE * (cond - uncond)

        base = both(current)
        heads1 = gather_heads(both(mixed1).astype(jnp.bfloat16))
        summed = jnp.concatenate(
            [jnp.dot(heads1, out_cols[k], preferred_element_type=jnp.float32) for k in range(2)],
            axis=1,
        )
        result = (base + summed).astype(jnp.bfloat16)
        guided = jnp.where(
            section == 0, passed_along(result[: rows // 2], "section", 1), result[rows // 2 :]
        )
        keys = jnp.where(section == 0, keys0, keys1)
        values = jnp.where(section == 0, values0, values1)
        return (guided, keys[None, None], values[None, None])
    else:
        term = jnp.dot(mixed0, out_w, preferred_element_type=jnp.float32)
        summed = lax.psum_scatter(
            term.astype(jnp.bfloat16), "tp", scatter_dimension=1, tiled=True
        ).astype(jnp.float32)
        current = lax.dynamic_slice_in_dim(entry, tp_index * local_width, local_width, 1)
        second = (current.astype(jnp.float32) + summed).astype(jnp.bfloat16)
        current = passed_along(second, "section", 1)
        second = lax.all_gather(current, "tp", axis=1, tiled=True)
        query1, keys1, values1 = project(second)
        mixed1 = attend_rows(query1, keys1, values1, old_keys, old_values, fresh_open, stale_open)
        term = jnp.dot(mixed1, out_w, preferred_element_type=jnp.float32)
        summed = lax.psum_scatter(
            term.astype(jnp.bfloat16), "tp", scatter_dimension=1, tiled=True
        ).astype(jnp.float32)
    result = (current.astype(jnp.float32) + summed).astype(jnp.bfloat16)
    quarter = seq_len // 4

    def rows_of(block):
        return lax.dynamic_slice_in_dim(result, block * quarter, quarter, 0)

    pair = jnp.concatenate([rows_of(0), rows_of(2)], axis=0)
    pair = jnp.where(section == 1, jnp.concatenate([rows_of(1), rows_of(3)]), passed_along(pair, "section", 1))
    own_rows = lax.dynamic_slice_in_dim(pair, branch * quarter, quarter, 0)
    outbound = lax.dynamic_slice_in_dim(pair, (1 - branch) * quarter, quarter, 0)
    partner = partner_2(outbound, "cfg", 0)
    conditioned = jnp.where(branch == 0, own_rows, partner).astype(jnp.float32)
    unconditioned = jnp.where(branch == 0, partner, own_rows).astype(jnp.float32)
    guided = (unconditioned + GUIDE_SCALE * (conditioned - unconditioned)).astype(jnp.bfloat16)
    keys = jnp.where(section == 0, keys0, keys1)
    values = jnp.where(section == 0, values0, values1)
    return (guided, keys[None, None], values[None, None])


def solution(mesh):
    placed = (
        P(),
        P("cfg", None),
        P("section", None),
        P("section", None, "tp"),
        P("section", None, "tp"),
        P("section", None, "tp"),
        P("section", "tp", None),
        P("cfg", "section", None, "tp"),
        P("cfg", "section", None, "tp"),
        P(),
        P(),
    )
    return jax.shard_map(
        body,
        mesh=mesh,
        in_specs=placed,
        out_specs=(
            P(("cfg", "section"), "tp"),
            P("cfg", "section", None, "tp"),
            P("cfg", "section", None, "tp"),
        ),
        check_vma=False,
    )
```

```python
import jax
import jax.numpy as jnp
from jax import lax
from jax.experimental import pallas as pl
from jax.experimental.pallas import tpu as pltpu
from jax.sharding import PartitionSpec as P

HEAD_DIM = 128
PATCH_LEN = 128
PATCHES = 4


GUIDE_SCALE = 3.0
NORM_EPS = 1e-06


def passed_along(block, axis, distance):
    devices = range(lax.axis_size(axis))
    route = [((i - distance) % len(devices), i) for i in devices]
    return lax.ppermute(block, axis, route)


def partner_2(x, axis, stride):
    return lax.ppermute(x, axis, [(i, i ^ 1 << stride) for i in range(lax.axis_size(axis))])


def attend_rows(query, fresh_keys, fresh_values, old_keys, old_values, fresh_open, stale_open):
    row_count = query.shape[0]
    head_count = query.shape[1] // HEAD_DIM
    key_count = fresh_keys.shape[0]
    factor = HEAD_DIM ** (-0.5)
    query_heads = query.reshape(row_count, head_count, HEAD_DIM)

    def split(array):
        return array.reshape(key_count, head_count, HEAD_DIM)

    fresh_scores = (
        jnp.einsum(
            "rhe,she->hrs", query_heads, split(fresh_keys), preferred_element_type=jnp.float32
        )
        * factor
    )
    old_scores = (
        jnp.einsum("rhe,she->hrs", query_heads, split(old_keys), preferred_element_type=jnp.float32)
        * factor
    )
    fresh_scores = jnp.where(fresh_open[None], fresh_scores, -jnp.inf)
    old_scores = jnp.where(stale_open[None], old_scores, -jnp.inf)
    top = jnp.maximum(
        jnp.max(fresh_scores, axis=2, keepdims=True), jnp.max(old_scores, axis=2, keepdims=True)
    )
    fresh_exp = jnp.exp(fresh_scores - top)
    old_exp = jnp.exp(old_scores - top)
    total = jnp.sum(fresh_exp, axis=2, keepdims=True) + jnp.sum(old_exp, axis=2, keepdims=True)
    fresh_weight = (fresh_exp / total).astype(jnp.bfloat16)
    old_weight = (old_exp / total).astype(jnp.bfloat16)
    mixed = jnp.einsum(
        "hrs,she->rhe", fresh_weight, split(fresh_values), preferred_element_type=jnp.float32
    )
    mixed = mixed + jnp.einsum(
        "hrs,she->rhe", old_weight, split(old_values), preferred_element_type=jnp.float32
    )
    return mixed.reshape(row_count, head_count * HEAD_DIM).astype(jnp.bfloat16)


GRID_X = 2
LINE = 4
CUTS = 4
MESH = pl.DeviceIdType.MESH


def span(index, size):
    return pl.ds(pl.multiple_of(index * size, size), size)


def arrived(ref, sem):
    pltpu.make_async_copy(ref, ref, sem).wait()


def greet(targets):
    barrier = pltpu.get_barrier_semaphore()
    for target in targets:
        pl.semaphore_signal(barrier, inc=1, device_id=target, device_id_type=MESH)
    pl.semaphore_wait(barrier, len(targets))


def send(src, dst, send_sem, recv_sem, target):
    copy = pltpu.make_async_remote_copy(
        src_ref=src,
        dst_ref=dst,
        send_sem=send_sem,
        recv_sem=recv_sem,
        device_id=target,
        device_id_type=MESH,
    )
    copy.start()
    return copy


def share_kernel(
    w_out,
    w_query,
    w_key,
    w_value,
    mixed,
    wo,
    heads,
    proj,
    cols,
    wo_recv,
    wo_send,
    heads_recv,
    heads_send,
    proj_recv,
    proj_send,
    cols_recv,
    cols_send,
    edge_sem,
    local_sem,
):
    c = lax.axis_index("cfg")
    s = lax.axis_index("section")
    t = lax.axis_index("tp")
    tp = GRID_X * LINE
    half = wo.shape[1]
    part = half // 2
    head = mixed.shape[1]
    slim = cols.shape[2]
    across = t + 1 - 2 * lax.rem(t, 2)
    peers = [lax.rem(t + GRID_X * k, tp) for k in range(1, LINE)]
    sibling = {"cfg": 1 - c}
    other = {"section": 1 - s}
    greet([{"tp": lax.rem(t + k, tp)} for k in range(1, tp)] + [sibling, other])
    weights = (w_query, w_key, w_value)

    def wo_at(core, index):
        return wo.at[span(index, head), span(core, part)]

    piece = part // CUTS

    def wo_cut(core, index, cut):
        return wo.at[span(index, head), span(core * CUTS + cut, piece)]

    def heads_at(index):
        return heads.at[index]

    def cols_at(core, index):
        return cols.at[core, span(index, head), :]

    def proj_at(core, j):
        return proj.at[j, span(core, part), :]

    def edge(j):
        return edge_sem.at[j]

    first_head = (mixed, heads_at(t))
    first_wo = (w_out.at[:, span(c, part)], wo_at(c, t))

    @pl.when(s == 0)
    def _():
        send(mixed, heads_at(t), edge(0), heads_recv.at[t], other)
        for cut in range(CUTS):
            send(
                w_out.at[:, span((c + 2) * CUTS + cut, piece)],
                wo_cut(c, t, cut),
                edge(1 + cut),
                wo_recv.at[c, t, cut],
                other,
            )
        a = pltpu.make_async_copy(*first_head, local_sem.at[0])
        b = pltpu.make_async_copy(*first_wo, local_sem.at[1])
        a.start()
        b.start()
        a.wait()
        b.wait()

    def own_copies():
        copies = [
            pltpu.make_async_copy(
                w.at[half : 2 * half, :], proj.at[j], local_sem.at[j]
            )
            for j, w in enumerate(weights)
        ]
        copies += [
            pltpu.make_async_copy(
                w_out.at[:, pl.ds(pl.multiple_of(2 * slim * t + slim * core, slim), slim)],
                cols_at(core, t),
                local_sem.at[3 + core],
            )
            for core in range(2)
        ]
        return copies

    @pl.when(s == 1)
    def _():
        for j, w in enumerate(weights):
            send(w.at[span(c, part), :], proj_at(c, j), edge(j), proj_recv.at[c, j], other)
        for k in range(1, tp):
            to = lax.rem(t + k, tp)
            send(
                w_out.at[:, pl.ds(pl.multiple_of(2 * slim * to + slim * c, slim), slim)],
                cols_at(c, t),
                cols_send.at[k],
                cols_recv.at[c, t],
                {"tp": to},
            )
        for copy in own_copies():
            copy.start()
        arrived(heads_at(t), heads_recv.at[t])

    pending = []

    def pass_heads(index, slot, target):
        pending.append(
            send(heads_at(index), heads_at(index), heads_send.at[slot], heads_recv.at[index], target)
        )

    def pass_wo(index, slot, cut, target):
        pending.append(
            send(
                wo_cut(c, index, cut),
                wo_cut(c, index, cut),
                wo_send.at[slot, cut],
                wo_recv.at[c, index, cut],
                target,
            )
        )

    def take_wo(index, cut):
        arrived(wo_cut(c, index, cut), wo_recv.at[c, index, cut])

    for k, peer in enumerate(peers):
        pass_heads(t, k, {"tp": peer})
    pass_heads(t, 3, {"tp": across})
    for cut in range(CUTS):

        @pl.when(s == 1)
        def _():
            take_wo(t, cut)

        pass_wo(t, 3, cut, {"tp": across})
        for k, peer in enumerate(peers):
            pass_wo(t, k, cut, {"tp": peer})
    for k in (2, 0, 1):
        peer = peers[k]
        arrived(heads_at(peer), heads_recv.at[peer])
        pass_heads(peer, 4 + k, {"tp": across})

    def finish(cut):
        for k in range(LINE):
            index = lax.rem(across + GRID_X * k, tp)
            take_wo(index, cut)
            pass_wo(index, 11 + k, cut, sibling)

    for cut in range(CUTS):
        for k in (2, 0, 1):
            take_wo(peers[k], cut)
            pass_wo(peers[k], 4 + k, cut, {"tp": across})
        pass_wo(t, 7, cut, sibling)
        for k in range(LINE - 1):
            pass_wo(peers[k], 8 + k, cut, sibling)
        if cut > 0:
            finish(cut - 1)
    finish(CUTS - 1)
    for k in range(LINE):
        index = lax.rem(across + GRID_X * k, tp)
        arrived(heads_at(index), heads_recv.at[index])

    @pl.when(s == 0)
    def _():
        for j in range(3):
            arrived(proj_at(c, j), proj_recv.at[c, j])
            send(proj_at(c, j), proj_at(c, j), proj_send.at[j], proj_recv.at[c, j], sibling)
        for j in range(3):
            arrived(proj_at(1 - c, j), proj_recv.at[1 - c, j])
            arrived(proj_at(c, j), proj_send.at[j])
        arrived(mixed, edge(0))
        for cut in range(CUTS):
            arrived(wo_cut(c, t, cut), edge(1 + cut))

    @pl.when(s == 1)
    def _():
        for k in range(1, tp):
            index = lax.rem(t + k, tp)
            arrived(cols_at(c, index), cols_recv.at[c, index])
            send(
                cols_at(c, index),
                cols_at(c, index),
                cols_send.at[tp + k],
                cols_recv.at[c, index],
                sibling,
            )
        for k in range(1, tp):
            index = lax.rem(t + k, tp)
            arrived(cols_at(1 - c, index), cols_recv.at[1 - c, index])
            arrived(cols_at(c, index), cols_send.at[k])
            arrived(cols_at(c, index), cols_send.at[tp + k])
        for j, w in enumerate(weights):
            arrived(w.at[span(c, part), :], edge(j))
        for copy in own_copies():
            copy.wait()

    for k in range(tp):
        for cut in range(CUTS):
            arrived(wo_cut(1 - c, k, cut), wo_recv.at[1 - c, k, cut])
    for copy in pending:
        copy.wait_send()


def share(w_out, w_query, w_key, w_value, mixed):
    head, width = w_out.shape
    tp = GRID_X * LINE
    kind = w_out.dtype
    DMA = pltpu.SemaphoreType.DMA
    any_spec = pl.BlockSpec(memory_space=pl.ANY)
    return pl.pallas_call(
        share_kernel,
        out_shape=(
            jax.ShapeDtypeStruct((tp * head, width // 2), kind),
            jax.ShapeDtypeStruct((tp,) + mixed.shape, kind),
            jax.ShapeDtypeStruct((3, width // 2, head), kind),
            jax.ShapeDtypeStruct((2, tp * head, width // tp // 2), kind),
        ),
        in_specs=[any_spec] * 5,
        out_specs=(any_spec,) * 4,
        scratch_shapes=[
            DMA((2, tp, CUTS)),
            DMA((16, CUTS)),
            DMA((tp,)),
            DMA((8,)),
            DMA((2, 3)),
            DMA((3,)),
            DMA((2, tp)),
            DMA((2 * tp,)),
            DMA((max(3, 1 + CUTS),)),
            DMA((5,)),
        ],
        compiler_params=pltpu.CompilerParams(collective_id=0, has_side_effects=True),
    )(w_out, w_query, w_key, w_value, mixed)


def gather_kernel(mixed, heads, recv, sent, local_sem):
    t = lax.axis_index("tp")
    tp = GRID_X * LINE
    head = mixed.shape[1]
    across = t + 1 - 2 * lax.rem(t, 2)
    peers = [lax.rem(t + GRID_X * k, tp) for k in range(1, LINE)]
    greet([{"tp": p} for p in peers] + [{"tp": across}])

    def heads_at(index):
        return heads.at[:, span(index, head)]

    local = pltpu.make_async_copy(mixed, heads_at(t), local_sem)
    local.start()
    pending = []
    for k, peer in enumerate(peers):
        pending.append(send(mixed, heads_at(t), sent.at[k], recv.at[t], {"tp": peer}))
    pending.append(send(mixed, heads_at(t), sent.at[3], recv.at[t], {"tp": across}))
    for k in (2, 0, 1):
        peer = peers[k]
        arrived(heads_at(peer), recv.at[peer])
        pending.append(
            send(heads_at(peer), heads_at(peer), sent.at[4 + k], recv.at[peer], {"tp": across})
        )
    for k in range(LINE):
        index = lax.rem(across + GRID_X * k, tp)
        arrived(heads_at(index), recv.at[index])
    local.wait()
    for copy in pending:
        copy.wait_send()


def gather_heads(mixed):
    tp = GRID_X * LINE
    DMA = pltpu.SemaphoreType.DMA
    return pl.pallas_call(
        gather_kernel,
        out_shape=jax.ShapeDtypeStruct((mixed.shape[0], tp * mixed.shape[1]), mixed.dtype),
        in_specs=[pl.BlockSpec(memory_space=pltpu.VMEM)],
        out_specs=pl.BlockSpec(memory_space=pltpu.VMEM),
        scratch_shapes=[DMA((tp,)), DMA((8,)), DMA],
        compiler_params=pltpu.CompilerParams(
            collective_id=1, has_side_effects=True, vmem_limit_bytes=16 * 1024 * 1024
        ),
    )(mixed)


def body(
    latent,
    condition,
    gain,
    w_query,
    w_key,
    w_value,
    w_out,
    stale_keys,
    stale_values,
    patch_order,
    stale_mask,
):
    tp_count = lax.axis_size("tp")
    section_count = lax.axis_size("section")
    section = lax.axis_index("section")
    tp_index = lax.axis_index("tp")
    branch = lax.axis_index("cfg")
    width = latent.shape[1]
    local_width = width // tp_count
    seq_len = latent.shape[0]
    query_w = w_query[0]
    key_w = w_key[0]
    value_w = w_value[0]
    out_w = w_out[0]
    gain_row = gain[0].astype(jnp.float32)
    old_keys = stale_keys[0, 0]
    old_values = stale_values[0, 0]
    numbers = jnp.arange(PATCHES, dtype=jnp.int32)
    placed = jnp.sum(
        numbers[:, None] * (patch_order[:, None] == numbers[None, :]).astype(jnp.int32), axis=0
    )
    pos = jnp.repeat(placed, PATCH_LEN)
    key_open = jnp.repeat(stale_mask, PATCH_LEN) == 1
    fresh_open = pos[None, :] <= pos[:, None]
    stale_open = (pos[None, :] > pos[:, None]) & key_open[None, :]
    entry = (latent.astype(jnp.float32) + condition[0].astype(jnp.float32)[None, :]).astype(
        jnp.bfloat16
    )
    planned = tp_count == GRID_X * LINE

    def project(rows):
        row_float = rows.astype(jnp.float32)
        scaled = row_float * lax.rsqrt(
            jnp.mean(row_float * row_float, axis=1, keepdims=True) + NORM_EPS
        )
        normed = (scaled * gain_row[None, :]).astype(jnp.bfloat16)
        return [
            jnp.dot(normed, w, preferred_element_type=jnp.float32).astype(jnp.bfloat16)
            for w in (query_w, key_w, value_w)
        ]

    query0, keys0, values0 = project(entry)
    mixed0 = attend_rows(query0, keys0, values0, old_keys, old_values, fresh_open, stale_open)
    if planned:
        half = width // 2
        later_gain = jnp.where(section == 0, passed_along(gain[0], "section", 1), gain[0])
        half_gain = lax.dynamic_slice_in_dim(later_gain, section * half, half, 0)
        out_half, heads0, weights_half, out_cols = share(out_w, query_w, key_w, value_w, mixed0)
        entry_half = lax.dynamic_slice_in_dim(entry, section * half, half, 1)
        second = (
            entry_half.astype(jnp.float32)
            + jnp.dot(
                heads0.transpose(1, 0, 2).reshape(seq_len, tp_count * HEAD_DIM),
                out_half,
                preferred_element_type=jnp.float32,
            )
        ).astype(jnp.bfloat16)
        second_float = second.astype(jnp.float32)
        squares = jnp.sum(second_float * second_float, axis=1)
        geared = (second_float * half_gain.astype(jnp.float32)[None, :]).astype(jnp.bfloat16)
        partial = jnp.concatenate(
            [jnp.dot(geared, weights_half[j], preferred_element_type=jnp.float32) for j in range(3)],
            axis=1,
        )
        far_partial = passed_along(partial.astype(jnp.bfloat16), "section", 1)
        far_squares = passed_along(squares, "section", 1)
        scale = lax.rsqrt((squares + far_squares) / width + NORM_EPS)
        projected = ((partial + far_partial.astype(jnp.float32)) * scale[:, None]).astype(
            jnp.bfloat16
        )
        query1, keys1, values1 = jnp.split(projected, 3, axis=1)
        place = lax.rem(tp_index, tp_count // 2)
        current = lax.dynamic_slice_in_dim(second, place * local_width, local_width, 1)
        current = jnp.where(
            tp_index < tp_count // 2, passed_along(current, "section", 1), current
        )
        mixed1 = attend_rows(query1, keys1, values1, old_keys, old_values, fresh_open, stale_open)
        rows = seq_len // 2

        def both(array):
            mine = lax.dynamic_slice_in_dim(array, branch * rows, rows, 0)
            away = lax.dynamic_slice_in_dim(array, (1 - branch) * rows, rows, 0)
            away = partner_2(away, "cfg", 0).astype(jnp.float32)
            mine = mine.astype(jnp.float32)
            cond = jnp.where(branch == 0, mine, away)
            uncond = jnp.where(branch == 0, away, mine)
            return uncond + GUIDE_SCALE * (cond - uncond)

        base = both(current)
        heads1 = gather_heads(both(mixed1).astype(jnp.bfloat16))
        summed = jnp.concatenate(
            [jnp.dot(heads1, out_cols[k], preferred_element_type=jnp.float32) for k in range(2)],
            axis=1,
        )
        result = (base + summed).astype(jnp.bfloat16)
        guided = jnp.where(
            section == 0, passed_along(result[: rows // 2], "section", 1), result[rows // 2 :]
        )
        keys = jnp.where(section == 0, keys0, keys1)
        values = jnp.where(section == 0, values0, values1)
        return (guided, keys[None, None], values[None, None])
    else:
        term = jnp.dot(mixed0, out_w, preferred_element_type=jnp.float32)
        summed = lax.psum_scatter(
            term.astype(jnp.bfloat16), "tp", scatter_dimension=1, tiled=True
        ).astype(jnp.float32)
        current = lax.dynamic_slice_in_dim(entry, tp_index * local_width, local_width, 1)
        second = (current.astype(jnp.float32) + summed).astype(jnp.bfloat16)
        current = passed_along(second, "section", 1)
        second = lax.all_gather(current, "tp", axis=1, tiled=True)
        query1, keys1, values1 = project(second)
        mixed1 = attend_rows(query1, keys1, values1, old_keys, old_values, fresh_open, stale_open)
        term = jnp.dot(mixed1, out_w, preferred_element_type=jnp.float32)
        summed = lax.psum_scatter(
            term.astype(jnp.bfloat16), "tp", scatter_dimension=1, tiled=True
        ).astype(jnp.float32)
    result = (current.astype(jnp.float32) + summed).astype(jnp.bfloat16)
    quarter = seq_len // 4

    def rows_of(block):
        return lax.dynamic_slice_in_dim(result, block * quarter, quarter, 0)

    pair = jnp.concatenate([rows_of(0), rows_of(2)], axis=0)
    pair = jnp.where(section == 1, jnp.concatenate([rows_of(1), rows_of(3)]), passed_along(pair, "section", 1))
    own_rows = lax.dynamic_slice_in_dim(pair, branch * quarter, quarter, 0)
    outbound = lax.dynamic_slice_in_dim(pair, (1 - branch) * quarter, quarter, 0)
    partner = partner_2(outbound, "cfg", 0)
    conditioned = jnp.where(branch == 0, own_rows, partner).astype(jnp.float32)
    unconditioned = jnp.where(branch == 0, partner, own_rows).astype(jnp.float32)
    guided = (unconditioned + GUIDE_SCALE * (conditioned - unconditioned)).astype(jnp.bfloat16)
    keys = jnp.where(section == 0, keys0, keys1)
    values = jnp.where(section == 0, values0, values1)
    return (guided, keys[None, None], values[None, None])


def solution(mesh):
    placed = (
        P(),
        P("cfg", None),
        P("section", None),
        P("section", None, "tp"),
        P("section", None, "tp"),
        P("section", None, "tp"),
        P("section", "tp", None),
        P("cfg", "section", None, "tp"),
        P("cfg", "section", None, "tp"),
        P(),
        P(),
    )
    return jax.shard_map(
        body,
        mesh=mesh,
        in_specs=placed,
        out_specs=(
            P(("cfg", "section"), "tp"),
            P("cfg", "section", None, "tp"),
            P("cfg", "section", None, "tp"),
        ),
        check_vma=False,
    )
```
